256 devices in a mesh: seq: 128 (over x, y, z_lo, core), dp: 2 (over z_hi).
Axes of the slice: x: 4, y: 4, z: 8 (z_hi: 2, z_lo: 4; z = z_hi * 4 + z_lo), core: 2. Of those that a mesh axis runs over, the one named last changes fastest.
Arguments:
- inputs: bfloat16 [2, 16384, 1024], P('dp', 'seq'), may hold values from -6 to 6
- cotangent: bfloat16 [2, 16384, 1024], P('dp', 'seq'), may hold values from -6 to 6
- value_weight: bfloat16 [1024, 1024], replicated, may hold values from -0.1875 to 0.1875
- gate_weight: bfloat16 [1024, 1024], replicated, may hold values from -0.1875 to 0.1875
- filter_taps: bfloat16 [16384, 1024], P('seq'), as said below
Outputs:
- input_grad: bfloat16 [2, 16384, 1024], P('dp', 'seq')
- projection_grads: float32 [2048, 1024], P('seq', 'dp')
- filter_grad: float32 [16384, 1024], P('seq')
The draws below stay inside these ranges and needn't reach their ends.
Inputs may be any that keep to these rules, and one draw needn't show every extreme that they name: `filter_taps`: real filter taps of order 16384^(-1/2), independent over positions and channels.
All inputs are finite; a program needn't handle non-finite values.
Results may differ from the reference program's by a relative error of at most 0.014.
Values may be sent and summed in bfloat16 or wider, within the bound.
No kernel may reach another device: no remote copies, remote signals or barrier semaphores. Data moves between devices by JAX's collectives and lax.ppermute only.
A program may use at most 128 MiB of HBM per device.

```python
import jax
import jax.numpy as jnp

D = 1024
LENGTH = 16384
BATCH = 2
TOKENS = 32768


def draw_filter_taps(key, part):
    key = jax.random.fold_in(key, 7)
    first, second = jax.random.split(key)
    spread = jnp.exp(jax.random.uniform(second, (1, D), jnp.float32, -0.55, 0.55))
    base = jax.random.normal(first, (LENGTH, D), jnp.float32)
    return (base * spread * LENGTH ** (-0.5)).astype(jnp.bfloat16)


def block_scale(stream_key, dims, cuts, least, largest):
    def one(axis_at, parts):
        heights = jax.random.uniform(jax.random.fold_in(jax.random.fold_in(stream_key, 6), axis_at), (parts,), jnp.float32, least / len(cuts), largest / len(cuts))
        return jnp.repeat(jnp.exp(heights), dims[axis_at] // parts).reshape((-1,) + (1,) * (len(dims) - axis_at - 1))

    loudness = one(*cuts[0])
    for cut in cuts[1:]:
        loudness = loudness * one(*cut)
    return loudness


def noise(stream_key, extent, deviation, limit, cuts=(), kind=jnp.bfloat16):
    result = jax.random.normal(stream_key, extent, jnp.float32) * deviation
    if len(cuts) > 0:
        result = block_scale(stream_key, extent, cuts, -0.22, 0.18) * result
    return jnp.clip(result, min=-limit, max=limit).astype(kind)


def setup_inputs(seed: int = 0) -> dict:
    key_list = jax.random.split(jax.random.key(seed), 6)
    return {
        "inputs": noise(key_list[0], (BATCH, LENGTH, D), 1.0, 6.0, ((0, 2), (1, 128))),
        "cotangent": noise(key_list[1], (BATCH, LENGTH, D), 1.0, 6.0, ((0, 2), (1, 128))),
        "value_weight": noise(key_list[2], (D, D), D ** -0.5, 0.1875),
        "gate_weight": noise(key_list[3], (D, D), D ** -0.5, 0.1875),
        "filter_taps": draw_filter_taps(jax.random.fold_in(key_list[5], 71), 0),
    }


def spectrum(signal):
    return jnp.fft.rfft(signal.astype(jnp.float32), n=2 * LENGTH, axis=-2)


def restore(spec):
    return jnp.fft.irfft(spec, n=2 * LENGTH, axis=-2)[..., :LENGTH, :]


def reference(inputs, cotangent, value_weight, gate_weight, filter_taps):
    value = jnp.dot(inputs, value_weight, preferred_element_type=jnp.float32).astype(jnp.bfloat16)
    gate = jnp.dot(inputs, gate_weight, preferred_element_type=jnp.float32)
    filt = spectrum(filter_taps)
    vals = spectrum(value)
    flipped = vals[..., ::-1]
    mixed = restore(filt * vals + jnp.conj(filt) * flipped)
    cot = cotangent.astype(jnp.float32)
    gate_grad = (cot * mixed).astype(jnp.bfloat16)
    mix_grad = (cot * gate).astype(jnp.bfloat16)
    grads = spectrum(mix_grad)
    value_grad = restore(jnp.conj(filt) * grads + (filt * grads)[..., ::-1]).astype(jnp.bfloat16)
    input_grad = (jnp.dot(value_grad, value_weight.T, preferred_element_type=jnp.float32)
                  + jnp.dot(gate_grad, gate_weight.T, preferred_element_type=jnp.float32)).astype(jnp.bfloat16)
    scale = TOKENS ** -0.5
    joined = jnp.concatenate([value_grad, gate_grad], axis=-1).reshape(-1, 2 * D)
    flat_in = inputs.reshape(-1, D)
    projection_grads = jnp.dot(joined.T, flat_in, preferred_element_type=jnp.float32) * scale
    spec_grad = jnp.sum(jnp.conj(vals) * grads + jnp.conj(grads) * flipped, axis=0)
    filter_grad = restore(spec_grad) * scale
    return input_grad, projection_grads, filter_grad
```

```python
import math

import jax
import jax.numpy as jnp
import numpy as np
from jax import lax
from jax.experimental import pallas as pl
from jax.experimental.pallas import tpu as pltpu
from jax.sharding import Mesh, PartitionSpec as P

F32 = jnp.float32
BF16 = jnp.bfloat16
D = 1024
L = 16384
SIDE = 128
CHIPS = 64
ARRS = 3
ROWS = ARRS * 8
SEQ = ("x", "y", "z", "c")
RING = ("x", "y", "z")
VMEM = pl.BlockSpec(memory_space=pltpu.VMEM)
SMEM = pl.BlockSpec(memory_space=pltpu.SMEM)
PARAMS = pltpu.CompilerParams(vmem_limit_bytes=56 * 1024 * 1024)


def owned(core):
    chans = np.zeros((CHIPS, 8), np.int64)
    q = 4 * np.arange(CHIPS)[:, None] + np.arange(4)[None, :]
    chans[:, :4] = 32 * (q // 16) + 16 * core + q % 16
    chans[:, 4:] = D - 1 - chans[:, :4]
    return chans.reshape(-1)


def one_hot_rows(index, width):
    return (index[:, None] == np.arange(width)[None, :]).astype(jnp.bfloat16)


def channel_order():
    return np.stack([one_hot_rows(owned(core), D) for core in range(2)])


def block_order():
    chans = owned(0)
    order = []
    for m in range(32):
        half = 0 if m < 16 else 1
        for i in range(16):
            order.append(int(np.nonzero(chans == 32 * m + 16 * half + i)[0][0]))
    return one_hot_rows(np.array(order), 512)


def tables():
    k = np.arange(SIDE)
    quarter = k + 0.25
    outer = 2 * math.pi / SIDE * np.outer(quarter, k)
    both = np.concatenate([np.cos(outer), -np.sin(outer)], axis=0)
    swapped = both.reshape(2 * SIDE, CHIPS, 2)[:, :, ::-1].reshape(2 * SIDE, SIDE)
    outer_table = np.stack([both, swapped])
    twist = 2 * math.pi / L * np.outer(quarter, k)
    inner = 2 * math.pi / SIDE * np.outer(k, k)
    cos, sin = np.cos(inner), np.sin(inner)
    inner_table = np.block([[cos, -sin], [sin, cos]])
    return (
        outer_table.astype(jnp.bfloat16),
        outer_table.transpose(0, 2, 1).astype(jnp.bfloat16),
        np.cos(twist).astype(np.float32),
        np.sin(twist).astype(np.float32),
        inner_table.astype(jnp.bfloat16),
        inner_table.T.astype(jnp.bfloat16),
    )


def dot(a, b, ca=1, cb=0):
    return lax.dot_general(a, b, (((ca,), (cb,)), ((), ())), preferred_element_type=F32)


def project_kernel(core, inputs, cot, taps, value_w, gate_w, order, keep, give, cot_keep, cot_give):
    value = dot(inputs[...], value_w[...]).astype(BF16)
    gate = dot(inputs[...], gate_w[...])
    mix = (cot[...].astype(F32) * gate).astype(BF16)
    stacked = jnp.concatenate([value, mix, taps[...], cot[...]], axis=0)
    for side, (out, cot_out) in enumerate(((keep, cot_keep), (give, cot_give))):
        pick = order[core[0] ^ side]
        moved = dot(pick, stacked, 1, 1)
        parts = [moved[:, a * SIDE:(a + 1) * SIDE].reshape(CHIPS, 8, SIDE) for a in range(3)]
        out[...] = jnp.concatenate(parts, axis=1).reshape(CHIPS * ROWS, SIDE).astype(BF16)
        cot_out[...] = moved[:, 3 * SIDE:].astype(BF16)


def convolve_kernel(core, signal, outer, outer_t, tw_re, tw_im, inner, inner_t, result, flat, spec):
    flat[...] = signal[...].astype(F32)
    outer_m = outer[core[0]]
    outer_tm = outer_t[core[0]]
    cos = tw_re[...]
    sin = tw_im[...]
    inner_m = inner[...]
    inner_tm = inner_t[...]

    for j in range(ROWS):
        sig = flat[pl.ds(j, SIDE, stride=ROWS), :].astype(BF16)
        part = dot(outer_m, sig)
        re, im = part[:SIDE], part[SIDE:]
        turned = jnp.concatenate([re * cos + im * sin, im * cos - re * sin], axis=1)
        spec[j] = dot(turned.astype(BF16), inner_m)

    def back(j, re, im):
        both = jnp.concatenate([re, im], axis=1).astype(BF16)
        part = dot(both, inner_tm)
        re, im = part[:, :SIDE], part[:, SIDE:]
        turned = jnp.concatenate([re * cos - im * sin, re * sin + im * cos], axis=0)
        out = dot(outer_tm, turned.astype(BF16))
        flat[pl.ds(j, SIDE, stride=ROWS), :] = out * (1.0 / L)

    def mul(a, b):
        return (a[0] * b[0] - a[1] * b[1], a[0] * b[1] + a[1] * b[0])

    def mulc(a, b):
        return (a[0] * b[0] + a[1] * b[1], a[0] * b[1] - a[1] * b[0])

    def add(a, b):
        return (a[0] + b[0], a[1] + b[1])

    def load(j):
        both = spec[j]
        return (both[:, :SIDE], both[:, SIDE:])

    for s in range(8):
        t = (s + 4) % 8
        vals, grads, filt = load(s), load(8 + s), load(16 + s)
        vals_f, grads_f, filt_f = load(t), load(8 + t), load(16 + t)
        back(s, *add(mul(filt, vals), mulc(filt, vals_f)))
        back(8 + s, *add(mulc(filt, grads), mul(filt_f, grads_f)))
        back(16 + s, *add(mulc(vals, grads), mulc(grads, vals_f)))
    result[...] = flat[...].astype(BF16)


def weights_kernel(home, cot_own, cot_other, in_own, in_other, blocks, partial):
    full = home[...].astype(F32).reshape(CHIPS, 2 * ROWS, SIDE)
    sides = []
    for side, cot in ((0, cot_own), (1, cot_other)):
        base = side * ROWS
        mixed = full[:, base:base + 8].reshape(512, SIDE)
        grad = full[:, base + 8:base + 16].reshape(512, SIDE).astype(BF16)
        gated = (mixed * cot[...].astype(F32)).astype(BF16)
        sides.append((grad, gated))
    for a in range(2):
        rows = jnp.concatenate([sides[0][a], sides[1][a]], axis=1)
        rows = dot(blocks[...], rows).astype(BF16)
        total = dot(rows[:, :SIDE], in_own[...]) + dot(rows[:, SIDE:], in_other[...])
        partial[a * 512:(a + 1) * 512, :] = total.astype(BF16)


def inputs_kernel(core, own, other, cot, value_w, gate_w, order, input_grad, filter_part):
    near = own[...].astype(F32).reshape(CHIPS, ROWS, SIDE)
    far = other[...].astype(F32).reshape(CHIPS, ROWS, SIDE)
    natural = 0.0
    for side, full in ((0, near), (1, far)):
        stacked = jnp.concatenate(
            [full[:, a * 8:(a + 1) * 8].reshape(512, SIDE) for a in range(3)], axis=1
        ).astype(BF16)
        natural = natural + dot(stacked, order[core[0] ^ side], 0, 0)
    gated = (natural[:SIDE] * cot[...].astype(F32)).astype(BF16)
    grad = natural[SIDE:2 * SIDE].astype(BF16)
    filter_part[...] = natural[2 * SIDE:].astype(BF16)
    total = dot(grad, value_w[...], 1, 1) + dot(gated, gate_w[...], 1, 1)
    input_grad[...] = total.astype(BF16)


def shape(rows, cols, kind=BF16):
    return jax.ShapeDtypeStruct((rows, cols), kind)


def swap_cores(a):
    return lax.ppermute(a, "c", [(0, 1), (1, 0)])


def local(inputs, cotangent, value_weight, gate_weight, filter_taps):
    core = lax.axis_index("c").astype(jnp.int32).reshape(1)
    order = jnp.asarray(channel_order())
    flat_in = inputs.reshape(SIDE, D)
    cot = cotangent.reshape(SIDE, D)
    scale = float(2 * L) ** (-0.5)

    keep, give, cot_keep, cot_give = pl.pallas_call(
        project_kernel,
        out_shape=[shape(CHIPS * ROWS, SIDE)] * 2 + [shape(512, SIDE)] * 2,
        in_specs=[SMEM] + [VMEM] * 6,
        out_specs=[VMEM] * 4,
        compiler_params=PARAMS,
        name="project",
    )(core, flat_in, cot, filter_taps, value_weight, gate_weight, order)
    got = swap_cores(give)
    message = jnp.concatenate(
        [keep.reshape(CHIPS, ROWS, SIDE), got.reshape(CHIPS, ROWS, SIDE)], axis=1
    )
    spread = lax.all_to_all(message, RING, 0, 0, tiled=True)
    in_other = swap_cores(flat_in)
    cot_other = swap_cores(cot_give)

    result = pl.pallas_call(
        convolve_kernel,
        out_shape=shape(2 * CHIPS * ROWS, SIDE),
        in_specs=[SMEM] + [VMEM] * 7,
        out_specs=VMEM,
        scratch_shapes=[
            pltpu.VMEM((2 * CHIPS * ROWS, SIDE), F32),
            pltpu.VMEM((ROWS, SIDE, 2 * SIDE), F32),
        ],
        compiler_params=PARAMS,
        name="convolve",
    )(core, spread.reshape(2 * CHIPS * ROWS, SIDE), *[jnp.asarray(t) for t in tables()])
    home = lax.all_to_all(result.reshape(CHIPS, 2 * ROWS, SIDE), RING, 0, 0, tiled=True)

    partial = pl.pallas_call(
        weights_kernel,
        out_shape=shape(D, D),
        in_specs=[VMEM] * 6,
        out_specs=VMEM,
        compiler_params=PARAMS,
        name="weights",
    )(home.reshape(2 * CHIPS * ROWS, SIDE), cot_keep, cot_other, flat_in, in_other, jnp.asarray(block_order()))
    far = swap_cores(home[:, ROWS:].reshape(CHIPS * ROWS, SIDE))
    pieces = lax.all_to_all(partial, ("x", "y"), 0, 0, tiled=True)

    input_grad, filter_part = pl.pallas_call(
        inputs_kernel,
        out_shape=[shape(SIDE, D), shape(SIDE, D)],
        in_specs=[SMEM] + [VMEM] * 6,
        out_specs=[VMEM] * 2,
        compiler_params=PARAMS,
        name="input_grad",
    )(core, home[:, :ROWS].reshape(CHIPS * ROWS, SIDE), far, cot, value_weight, gate_weight, order)
    filter_other = lax.ppermute(filter_part, "dp", [(0, 1), (1, 0)])
    filter_grad = (filter_part.astype(F32) + filter_other.astype(F32)) * scale

    sums = jnp.sum(pieces.reshape(16, 64, D).astype(F32), axis=0).astype(BF16)
    sums = sums.reshape(4, 16, 2, 512).transpose(0, 2, 1, 3).reshape(8, 16, 512)
    final = lax.all_to_all(sums, ("z", "dp"), 0, 0, tiled=True)
    rows = jnp.sum(final.astype(F32), axis=0) * scale
    pairs = [(2 * x + c, 2 * x + (c ^ (x & 1))) for x in range(4) for c in range(2)]
    projection_grads = lax.ppermute(rows, ("x", "c"), pairs)
    return (input_grad.reshape(1, SIDE, D), projection_grads, filter_grad)


def solution(mesh):
    fine = Mesh(mesh.devices.reshape(4, 4, 4, 2, 2), ("x", "y", "z", "c", "dp"))
    in_specs = (P("dp", SEQ, None), P("dp", SEQ, None), P(), P(), P(SEQ, None))
    out_specs = (P("dp", SEQ, None), P(SEQ, "dp"), P(SEQ, None))
    return jax.shard_map(local, mesh=fine, in_specs=in_specs, out_specs=out_specs, check_vma=False)
```

```python
import math

import jax
import jax.numpy as jnp
import numpy as np
from jax import lax
from jax.experimental import pallas as pl
from jax.experimental.pallas import tpu as pltpu
from jax.sharding import Mesh, PartitionSpec as P

F32 = jnp.float32
BF16 = jnp.bfloat16
D = 1024
L = 16384
SCALE = float(2 * L) ** (-0.5)
SIDE = 128
CHIPS = 64
ARRS = 3
ROWS = ARRS * 8
SEQ = ("x", "y", "z", "c")
RING = ("x", "y", "z")
VMEM = pl.BlockSpec(memory_space=pltpu.VMEM)
SMEM = pl.BlockSpec(memory_space=pltpu.SMEM)
PARAMS = pltpu.CompilerParams(vmem_limit_bytes=56 * 1024 * 1024)


def owned(z, core):
    chans = np.zeros((16, 8), np.int64)
    q = 4 * np.arange(16)[:, None] + np.arange(4)[None, :]
    chans[:, :4] = 128 * (q // 16) + 32 * z + 16 * core + q % 16
    chans[:, 4:] = D - 1 - chans[:, :4]
    return chans.reshape(-1)


def one_hot_rows(index, width):
    return (index[:, None] == np.arange(width)[None, :]).astype(jnp.bfloat16)


def channel_order():
    return np.stack(
        [
            np.concatenate([one_hot_rows(owned(z, core), D) for z in range(4)])
            for core in range(2)
        ]
    )


def block_order():
    chans = owned(0, 0)
    order = []
    for half in range(2):
        for y in range(4):
            for i in range(16):
                chan = 128 * y + i if half == 0 else 512 + 128 * y + 96 + 16 + i
                order.append(int(np.nonzero(chans == chan)[0][0]))
    return one_hot_rows(np.array(order), SIDE)


def tables():
    k = np.arange(SIDE)
    quarter = k + 0.25
    outer = 2 * math.pi / SIDE * np.outer(quarter, k)
    both = np.concatenate([np.cos(outer), -np.sin(outer)], axis=0)
    there = np.stack([both[:, k ^ core] for core in range(2)])
    back = []
    for z in range(4):
        for core in range(2):
            rows = []
            for xy in range(16):
                for step in range(4):
                    for slot in range(2):
                        rows.append(2 * (4 * xy + (z ^ step)) + (slot ^ core))
            back.append(both.T[np.array(rows)])
    twist = 2 * math.pi / L * np.outer(quarter, k)
    inner = 2 * math.pi / SIDE * np.outer(k, k)
    cos, sin = np.cos(inner), np.sin(inner)
    inner_table = np.block([[cos, -sin], [sin, cos]])
    return (
        there.astype(jnp.bfloat16),
        np.stack(back).astype(jnp.bfloat16),
        np.cos(twist).astype(np.float32),
        np.sin(twist).astype(np.float32),
        inner_table.astype(jnp.bfloat16),
        inner_table.T.astype(jnp.bfloat16),
    )


def dot(a, b, ca=1, cb=0):
    return lax.dot_general(a, b, (((ca,), (cb,)), ((), ())), preferred_element_type=F32)


def project_kernel(where, inputs, cot, taps, value_w, gate_w, order, keep, give, cot_keep, cot_give):
    z, core = where[0], where[1]
    value = dot(inputs[...], value_w[...]).astype(BF16)
    gate = dot(inputs[...], gate_w[...])
    mix = (cot[...].astype(F32) * gate).astype(BF16)
    stacked = jnp.concatenate([value, mix, taps[...], cot[...]], axis=0)
    for side, (out, cot_out) in enumerate(((keep, cot_keep), (give, cot_give))):
        moved = dot(order[core ^ side], stacked, 1, 1)
        lines = []
        for own in range(4):
            line = moved[own * SIDE:(own + 1) * SIDE]
            parts = [line[:, a * SIDE:(a + 1) * SIDE].reshape(16, 8, SIDE) for a in range(3)]
            lines.append(jnp.concatenate(parts, axis=1))
            cot_out[z ^ own] = line[:, 3 * SIDE:].astype(BF16)
        out[...] = jnp.concatenate(lines, axis=1).reshape(CHIPS * ROWS, SIDE).astype(BF16)


def convolve_kernel(where, signal, outer, outer_t, tw_re, tw_im, inner, inner_t, result, flat, spec):
    flat[...] = signal[...].astype(F32)
    outer_m = outer[where[1]]
    outer_tm = outer_t[2 * where[0] + where[1]]
    cos = tw_re[...]
    sin = tw_im[...]
    inner_m = inner[...]
    inner_tm = inner_t[...]

    for j in range(ROWS):
        sig = flat[pl.ds(j, SIDE, stride=ROWS), :].astype(BF16)
        part = dot(outer_m, sig)
        re, im = part[:SIDE], part[SIDE:]
        turned = jnp.concatenate([re * cos + im * sin, im * cos - re * sin], axis=1)
        spec[j] = dot(turned.astype(BF16), inner_m)

    def back(j, re, im):
        both = jnp.concatenate([re, im], axis=1).astype(BF16)
        part = dot(both, inner_tm)
        re, im = part[:, :SIDE], part[:, SIDE:]
        turned = jnp.concatenate([re * cos - im * sin, re * sin + im * cos], axis=0)
        out = dot(outer_tm, turned.astype(BF16))
        flat[pl.ds(j, SIDE, stride=ROWS), :] = out * (1.0 / L)

    def mul(a, b):
        return (a[0] * b[0] - a[1] * b[1], a[0] * b[1] + a[1] * b[0])

    def mulc(a, b):
        return (a[0] * b[0] + a[1] * b[1], a[0] * b[1] - a[1] * b[0])

    def add(a, b):
        return (a[0] + b[0], a[1] + b[1])

    def load(j):
        both = spec[j]
        return (both[:, :SIDE], both[:, SIDE:])

    for s in range(8):
        t = (s + 4) % 8
        vals, grads, filt = load(s), load(8 + s), load(16 + s)
        vals_f, grads_f, filt_f = load(t), load(8 + t), load(16 + t)
        back(s, *add(mul(filt, vals), mulc(filt, vals_f)))
        back(8 + s, *add(mulc(filt, grads), mul(filt_f, grads_f)))
        back(16 + s, *add(mulc(vals, grads), mulc(grads, vals_f)))
    result[...] = flat[...].astype(BF16)


def weights_kernel(home, blocks, *refs):
    cots, ins, partial = refs[:8], refs[8:16], refs[16]
    full = home[...].astype(F32).reshape(16, 8 * ROWS, SIDE)
    grads, gates = [], []
    for p in range(8):
        base = p * ROWS
        mixed = full[:, base:base + 8].reshape(SIDE, SIDE)
        grads.append(full[:, base + 8:base + 16].reshape(SIDE, SIDE).astype(BF16))
        gates.append((mixed * cots[p][...].astype(F32)).astype(BF16))
    joined = []
    for group in (grads, gates):
        joined.append(dot(blocks[...], jnp.concatenate(group, axis=1)).astype(BF16))
    joined = jnp.concatenate(joined, axis=0)
    total = dot(joined[:, :SIDE], ins[0][...])
    for p in range(1, 8):
        total = total + dot(joined[:, p * SIDE:(p + 1) * SIDE], ins[p][...])
    partial[...] = total.astype(BF16)


def inputs_kernel(where, cot, value_w, gate_w, order, far, *refs):
    lines, cross = refs[:4], refs[4:8]
    input_grad, filter_grad, stack = refs[8:]
    z, core = where[0], where[1]
    other = far[...].astype(F32).reshape(4, 16, ROWS + 8, SIDE)
    for k in range(4):
        near = lines[k][...].astype(F32).reshape(16, 2 * ROWS, SIDE)
        extra = cross[k][...].astype(F32).reshape(16, 16, SIDE)
        for side in range(2):
            if side == 0:
                parts = [near[:, a * 8:(a + 1) * 8] for a in range(3)] + [extra[:, :8]]
            else:
                parts = [other[k, :, a * 8:(a + 1) * 8] for a in range(4)]
            parts = [part.reshape(SIDE, SIDE) for part in parts]
            stack[core ^ side, z ^ k] = jnp.concatenate(parts, axis=1).astype(BF16)
    natural = dot(stack[...].reshape(D, 4 * SIDE), order[...].reshape(D, D), 0, 0)
    gated = (natural[:SIDE] * cot[...].astype(F32)).astype(BF16)
    grad = natural[SIDE:2 * SIDE].astype(BF16)
    filter_grad[...] = (natural[2 * SIDE:3 * SIDE] + natural[3 * SIDE:]) * SCALE
    total = dot(grad, value_w[...], 1, 1) + dot(gated, gate_w[...], 1, 1)
    input_grad[...] = total.astype(BF16)


def shape(*dims, kind=BF16):
    return jax.ShapeDtypeStruct(dims, kind)


def swap_cores(a):
    return lax.ppermute(a, "c", [(0, 1), (1, 0)])


def along(a, k):
    return lax.ppermute(a, "z", [(z, z ^ k) for z in range(4)])


def across(a, k):
    pairs = [(2 * z + dp, 2 * (z ^ k) + 1 - dp) for z in range(4) for dp in range(2)]
    return lax.ppermute(a, ("z", "dp"), pairs)


def final_pairs(other):
    pairs = []
    for x in range(4):
        for z in range(4):
            for c in range(2):
                flip = x & 1
                z_to, c_to = (3 - z, 1 - c) if flip else (z, c)
                if other is None:
                    pairs.append(((x * 4 + z) * 2 + c, (x * 4 + z_to) * 2 + c_to))
                else:
                    for dp in range(2):
                        start = ((x * 4 + z) * 2 + c) * 2 + dp
                        pairs.append((start, ((x * 4 + z_to) * 2 + c_to) * 2 + 1 - dp))
    return pairs


def local(inputs, cotangent, value_weight, gate_weight, filter_taps):
    z = lax.axis_index("z").astype(jnp.int32)
    core = lax.axis_index("c").astype(jnp.int32)
    dp = lax.axis_index("dp")
    where = jnp.stack([z, core])
    order = jnp.asarray(channel_order())
    flat_in = inputs.reshape(SIDE, D)
    cot = cotangent.reshape(SIDE, D)

    keep, give, cot_keep, cot_give = pl.pallas_call(
        project_kernel,
        out_shape=[shape(CHIPS * ROWS, SIDE)] * 2 + [shape(4, SIDE, SIDE)] * 2,
        in_specs=[SMEM] + [VMEM] * 6,
        out_specs=[VMEM] * 4,
        compiler_params=PARAMS,
        name="project",
    )(where, flat_in, cot, filter_taps, value_weight, gate_weight, order)
    got = swap_cores(give)
    message = jnp.concatenate(
        [keep.reshape(CHIPS, ROWS, SIDE), got.reshape(CHIPS, ROWS, SIDE)], axis=1
    )
    spread = lax.all_to_all(message, RING, 0, 0, tiled=True)

    cot_other = swap_cores(cot_give)
    cots = [cot_keep[0], cot_other[0]]
    ins = [flat_in, swap_cores(flat_in)]
    for k in range(1, 4):
        pair = along(jnp.stack([cot_keep[k], cot_other[k]]), k)
        moved = along(flat_in, k)
        cots += [pair[0], pair[1]]
        ins += [moved, swap_cores(moved)]

    result = pl.pallas_call(
        convolve_kernel,
        out_shape=shape(2 * CHIPS * ROWS, SIDE),
        in_specs=[SMEM] + [VMEM] * 7,
        out_specs=VMEM,
        scratch_shapes=[
            pltpu.VMEM((2 * CHIPS * ROWS, SIDE), F32),
            pltpu.VMEM((ROWS, SIDE, 2 * SIDE), F32),
        ],
        compiler_params=PARAMS,
        name="convolve",
    )(where, spread.reshape(2 * CHIPS * ROWS, SIDE), *[jnp.asarray(t) for t in tables()])
    home = lax.all_to_all(result.reshape(16, 8 * ROWS, SIDE), ("x", "y"), 0, 0, tiled=True)

    by_step = home.reshape(16, 4, 2 * ROWS, SIDE)
    lines, cross = [], []
    for k in range(4):
        line = by_step[:, k]
        parts = jnp.concatenate([line[:, 16:24], line[:, 40:48]], axis=1)
        lines.append(line if k == 0 else along(line, k))
        cross.append(across(parts, k))

    partial = pl.pallas_call(
        weights_kernel,
        out_shape=shape(256, D),
        in_specs=[VMEM] * 18,
        out_specs=VMEM,
        compiler_params=PARAMS,
        name="weights",
    )(home.reshape(2 * CHIPS * ROWS, SIDE), jnp.asarray(block_order()), *cots, *ins)
    pieces = lax.all_to_all(partial, ("x", "y"), 0, 0, tiled=True)

    far = swap_cores(
        jnp.stack(
            [jnp.concatenate([lines[k][:, ROWS:], cross[k][:, 8:]], axis=1) for k in range(4)]
        )
    )
    input_grad, filter_grad = pl.pallas_call(
        inputs_kernel,
        out_shape=[shape(SIDE, D), shape(SIDE, D, kind=F32)],
        in_specs=[SMEM] + [VMEM] * 13,
        out_specs=[VMEM] * 2,
        scratch_shapes=[pltpu.VMEM((2, 4, SIDE, 4 * SIDE), BF16)],
        compiler_params=PARAMS,
        name="input_grad",
    )(
        where,
        cot,
        value_weight,
        gate_weight,
        order.reshape(2, 4, SIDE, D),
        far.reshape(4 * 16 * 32, SIDE),
        *[line.reshape(16 * 48, SIDE) for line in lines],
        *[part.reshape(16 * 16, SIDE) for part in cross],
    )

    sums = jnp.sum(pieces.reshape(16, 16, D).astype(F32), axis=0)
    mine = lax.dynamic_slice_in_dim(sums, dp * 512, 512, 1)
    theirs = lax.dynamic_slice_in_dim(sums, (1 - dp) * 512, 512, 1)
    mine = lax.ppermute(mine, ("x", "z", "c"), final_pairs(None))
    theirs = lax.ppermute(theirs, ("x", "z", "c", "dp"), final_pairs(1))
    projection_grads = (mine + theirs) * SCALE
    return (input_grad.reshape(1, SIDE, D), projection_grads, filter_grad)


def solution(mesh):
    fine = Mesh(mesh.devices.reshape(4, 4, 4, 2, 2), ("x", "y", "z", "c", "dp"))
    in_specs = (P("dp", SEQ, None), P("dp", SEQ, None), P(), P(), P(SEQ, None))
    out_specs = (P("dp", SEQ, None), P(SEQ, "dp"), P(SEQ, None))
    return jax.shard_map(local, mesh=fine, in_specs=in_specs, out_specs=out_specs, check_vma=False)
```

```python
import math

import jax
import jax.numpy as jnp
import numpy as np
from jax import lax
from jax.experimental import pallas as pl
from jax.experimental.pallas import tpu as pltpu
from jax.sharding import Mesh, PartitionSpec as P

F32 = jnp.float32
BF16 = jnp.bfloat16
D = 1024
L = 16384
SCALE = float(2 * L) ** (-0.5)
SIDE = 128
CHIPS = 64
ARRS = 3
ROWS = ARRS * 8
SEQ = ("x", "y", "z", "c")
VMEM = pl.BlockSpec(memory_space=pltpu.VMEM)
SMEM = pl.BlockSpec(memory_space=pltpu.SMEM)


def one_hot_rows(index, width):
    return (index[:, None] == np.arange(width)[None, :]).astype(jnp.bfloat16)


def spread_order():
    orders = []
    for parity in range(2):
        index = []
        for y in range(4):
            for z in range(4):
                for core in range(2):
                    low = [32 * z + 16 * (core ^ parity) + 4 * y + s for s in range(4)]
                    index += low + [2 * SIDE - 1 - d for d in low]
        orders.append(one_hot_rows(np.array(index), 2 * SIDE))
    return np.stack(orders)


def classes(with_z):
    groups = []
    for dp in range(2):
        for core in range(2):
            members = [
                [((16 * x + 4 * y + z) * 2 + (core ^ (x & 1))) * 2 + dp for z in range(4)]
                for x in range(4)
                for y in range(4)
            ]
            if with_z:
                groups.append([member for row in members for member in row])
            else:
                groups += [[row[z] for row in members] for z in range(4)]
    return groups


def by_class(a, with_z):
    return lax.all_to_all(a, SEQ + ("dp",), 0, 0, axis_index_groups=classes(with_z), tiled=True)


def block_order():
    index = []
    for half in range(2):
        for y in range(4):
            for zz in range(4):
                for i in range(16):
                    x, z, q = (y, zz, i) if half == 0 else (3 - y, 3 - zz, 15 - i)
                    index.append((16 * x + 4 * (q // 4) + z) * 8 + 4 * half + q % 4)
    return one_hot_rows(np.array(index), 512)


def tables():
    k = np.arange(SIDE)
    quarter = k + 0.25
    outer = 2 * math.pi / SIDE * np.outer(quarter, k)
    both = np.concatenate([np.cos(outer), -np.sin(outer)], axis=0)
    back = []
    for core in range(2):
        rows = [2 * g + (slot ^ core ^ (g >> 4 & 1)) for g in range(CHIPS) for slot in range(2)]
        back.append(both.T[np.array(rows)])
    twist = 2 * math.pi / L * np.outer(quarter, k)
    inner = 2 * math.pi / SIDE * np.outer(k, k)
    cos, sin = np.cos(inner), np.sin(inner)
    inner_table = np.block([[cos, -sin], [sin, cos]])
    return (
        both.astype(jnp.bfloat16),
        np.stack(back).astype(jnp.bfloat16),
        np.cos(twist).astype(np.float32),
        np.sin(twist).astype(np.float32),
        inner_table.astype(jnp.bfloat16),
        inner_table.T.astype(jnp.bfloat16),
    )


def dot(a, b, ca=1, cb=0):
    return lax.dot_general(a, b, (((ca,), (cb,)), ((), ())), preferred_element_type=F32)


def project_kernel(core, inputs, cot, taps, order, value_w, gate_w, message, give, cot_own, w_buf, cot_buf, sems):
    fetch = [
        pltpu.make_async_copy(w, w_buf.at[i], sems.at[i]) for i, w in enumerate((value_w, gate_w))
    ]
    for copy in fetch:
        copy.start()
    for j in range(8):
        give[j * SIDE:(j + 1) * SIDE, :] = inputs[:, j * SIDE:(j + 1) * SIDE]
    fetch[0].wait()
    value = dot(inputs[...], w_buf[0]).astype(BF16)
    fetch[1].wait()
    gate = dot(inputs[...], w_buf[1])
    mix = (cot[...].astype(F32) * gate).astype(BF16)
    stacked = jnp.concatenate([value, mix, taps[...], cot[...]], axis=0)
    for b in range(4):
        low = stacked[:, b * SIDE:(b + 1) * SIDE]
        high = stacked[:, (7 - b) * SIDE:(8 - b) * SIDE]
        moved = dot(order[b & 1], jnp.concatenate([low, high], axis=1), 1, 1)
        parts = [moved[:, a * SIDE:(a + 1) * SIDE].reshape(32, 8, SIDE) for a in range(4)]
        block = jnp.concatenate(parts[:3], axis=1).reshape(32 * ROWS, SIDE).astype(BF16)
        message[b * 32 * ROWS:(b + 1) * 32 * ROWS, :] = block
        line = parts[3].reshape(16, 2, 8, SIDE)
        for c in range(2):
            rows = line[:, c ^ (b & 1)].reshape(SIDE, SIDE).astype(BF16)
            cot_buf[c ^ core[0], b * SIDE:(b + 1) * SIDE, :] = rows
    cot_own[...] = cot_buf[0]
    give[D:, :] = cot_buf[1]


def inverse(both, outer_tm, cos, sin, inner_tm):
    part = dot(both, inner_tm)
    re, im = part[:, :SIDE], part[:, SIDE:]
    turned = jnp.concatenate([re * cos - im * sin, re * sin + im * cos], axis=0)
    return dot(outer_tm, turned.astype(BF16)) * (1.0 / L)


def convolve_kernel(core, signal, outer, outer_t, tw_re, tw_im, inner, inner_t, result, flat, spec):
    flat[...] = signal[...].astype(F32)
    outer_m = outer[...]
    outer_tm = outer_t[core[0]]
    cos = tw_re[...]
    sin = tw_im[...]
    inner_m = inner[...]
    inner_tm = inner_t[...]

    for j in range(ROWS):
        sig = flat[pl.ds(j, SIDE, stride=ROWS), :].astype(BF16)
        part = dot(outer_m, sig)
        re, im = part[:SIDE], part[SIDE:]
        turned = jnp.concatenate([re * cos + im * sin, im * cos - re * sin], axis=1)
        spec[j] = dot(turned.astype(BF16), inner_m)

    def back(re, im):
        both = jnp.concatenate([re, im], axis=1).astype(BF16)
        return inverse(both, outer_tm, cos, sin, inner_tm)

    def mul(a, b):
        return (a[0] * b[0] - a[1] * b[1], a[0] * b[1] + a[1] * b[0])

    def mulc(a, b):
        return (a[0] * b[0] + a[1] * b[1], a[0] * b[1] - a[1] * b[0])

    def add(a, b):
        return (a[0] + b[0], a[1] + b[1])

    def load(j):
        both = spec[j]
        return (both[:, :SIDE], both[:, SIDE:])

    for s in range(8):
        t = (s + 4) % 8
        vals, grads, filt = load(s), load(8 + s), load(16 + s)
        vals_f, grads_f, filt_f = load(t), load(8 + t), load(16 + t)
        mixed = back(*add(mul(filt, vals), mulc(filt, vals_f)))
        flat[pl.ds(s, SIDE, stride=ROWS), :] = mixed
        grad = back(*add(mulc(filt, grads), mul(filt_f, grads_f)))
        flat[pl.ds(8 + s, SIDE, stride=ROWS), :] = grad
        part = add(mulc(vals, grads), mulc(grads, vals_f))
        flat[pl.ds(16 + s, SIDE, stride=ROWS), :] = back(*part)
    result[...] = flat[...].astype(BF16)


def weights_kernel(home, blocks, inputs, cot_own, got, partial):
    full = home[...].astype(F32).reshape(CHIPS, 2 * ROWS, SIDE)
    grads, gates = [], []
    for slot, cot in enumerate((cot_own[...], got[D:, :])):
        base = slot * ROWS
        mixed = full[:, base:base + 8].reshape(512, SIDE)
        grads.append(full[:, base + 8:base + 16].reshape(512, SIDE).astype(BF16))
        gates.append((mixed * cot.astype(F32)).astype(BF16))
    for a, group in enumerate((grads, gates)):
        rows = dot(blocks[...], jnp.concatenate(group, axis=1)).astype(BF16)
        for j in range(8):
            cols = slice(j * SIDE, (j + 1) * SIDE)
            pair = jnp.concatenate([inputs[:, cols], got[cols, :]], axis=0)
            partial[a * 512:(a + 1) * 512, cols] = dot(rows, pair).astype(BF16)


def natural_order(stack, order):
    width = stack.shape[3]
    low, high = [], []
    for b in range(4):
        rows = stack[16 * b:16 * b + 16].reshape(2 * SIDE, width).astype(BF16)
        both = dot(rows, order[0], 0, 0)
        low.append(both[:, :SIDE])
        high.insert(0, both[:, SIDE:])
    return jnp.concatenate(low + high, axis=1)


def inputs_kernel(core, cot, order, own, far, value_w, gate_w, input_grad, w_buf, stack, sems):
    fetch = [
        pltpu.make_async_copy(w, w_buf.at[i], sems.at[i]) for i, w in enumerate((value_w, gate_w))
    ]
    for copy in fetch:
        copy.start()
    for side, ref in ((0, own), (1, far)):
        full = ref[...].astype(F32).reshape(CHIPS, ROWS, SIDE)
        stack[:, core[0] ^ side] = jnp.concatenate([full[:, :8], full[:, 8:16]], axis=2)
    natural = natural_order(stack, order)
    gated = (natural[:SIDE] * cot[...].astype(F32)).astype(BF16)
    grad = natural[SIDE:].astype(BF16)
    fetch[0].wait()
    total = dot(grad, w_buf[0], 1, 1)
    fetch[1].wait()
    input_grad[...] = (total + dot(gated, w_buf[1], 1, 1)).astype(BF16)


def filter_kernel(core, order, mine, theirs, filter_grad, stack):
    total = (mine[...].astype(F32) + theirs[...].astype(F32)).reshape(2, CHIPS, 8, SIDE)
    for side in range(2):
        rounded = total[side].astype(BF16).astype(F32)
        stack[:, core[0] ^ side] = jnp.concatenate([rounded, total[side] - rounded], axis=2)
    both = natural_order(stack, order)
    filter_grad[...] = (both[:SIDE] + both[SIDE:]) * SCALE


def shape(*dims, kind=BF16):
    return jax.ShapeDtypeStruct(dims, kind)


def swap_cores(a):
    return lax.ppermute(a, "c", [(0, 1), (1, 0)])


def kernel(name, body, outs, ins, anys=0, scratch=(), gflop=0.1, mbyte=4.0, limit=24):
    return pl.pallas_call(
        body,
        out_shape=outs,
        in_specs=ins + [pl.BlockSpec(memory_space=pl.ANY)] * anys,
        out_specs=[VMEM] * len(outs),
        scratch_shapes=scratch,
        compiler_params=pltpu.CompilerParams(vmem_limit_bytes=limit * 2**20),
        cost_estimate=pl.CostEstimate(
            flops=int(gflop * 1e9), bytes_accessed=int(mbyte * 2**20), transcendentals=0
        ),
        name=name,
    )


def local(inputs, cotangent, value_weight, gate_weight, filter_taps):
    odd = lax.axis_index("x").astype(jnp.int32) & 1
    core = (lax.axis_index("c").astype(jnp.int32) ^ odd).reshape(1)
    order = jnp.asarray(spread_order())
    flat_in = inputs.reshape(SIDE, D)
    cot = cotangent.reshape(SIDE, D)
    w_scratch = pltpu.VMEM((2, D, D), BF16)
    sems = pltpu.SemaphoreType.DMA((2,))

    message, give, cot_own = kernel(
        "project",
        project_kernel,
        [shape(2 * CHIPS * ROWS, SIDE), shape(1536, SIDE), shape(512, SIDE)],
        [SMEM] + [VMEM] * 4,
        2,
        [w_scratch, pltpu.VMEM((2, 512, SIDE), BF16), sems],
        0.8,
        8.0,
        56,
    )(core, flat_in, cot, filter_taps, order, value_weight, gate_weight)
    spread = lax.all_to_all(message.reshape(2 * CHIPS, ROWS, SIDE), SEQ, 0, 0, tiled=True)
    got = swap_cores(give)

    (result,) = kernel(
        "convolve",
        convolve_kernel,
        [shape(2 * CHIPS * ROWS, SIDE)],
        [SMEM] + [VMEM] * 7,
        0,
        [
            pltpu.VMEM((2 * CHIPS * ROWS, SIDE), F32),
            pltpu.VMEM((ROWS, SIDE, 2 * SIDE), F32),
        ],
        1.2,
        4.0,
    )(core, spread.reshape(2 * CHIPS * ROWS, SIDE), *[jnp.asarray(t) for t in tables()])
    home = by_class(result.reshape(CHIPS, 2 * ROWS, SIDE), True)

    (partial,) = kernel(
        "weights", weights_kernel, [shape(D, D)], [VMEM] * 5, gflop=0.6, mbyte=4.0, limit=56
    )(home.reshape(2 * CHIPS * ROWS, SIDE), jnp.asarray(block_order()), flat_in, cot_own, got)
    parts = by_class(partial, False)

    own = home[:, :ROWS]
    far = swap_cores(home[:, ROWS:])
    filter_part = jnp.stack([own[:, 16:], far[:, 16:]]).reshape(1024, SIDE)
    filter_other = lax.ppermute(filter_part, "dp", [(0, 1), (1, 0)])
    (input_grad,) = kernel(
        "input_grad",
        inputs_kernel,
        [shape(SIDE, D)],
        [SMEM] + [VMEM] * 4,
        2,
        [w_scratch, pltpu.VMEM((CHIPS, 2, 8, 2 * SIDE), F32), sems],
        0.7,
        8.0,
        56,
    )(core, cot, order, own.reshape(1536, SIDE), far.reshape(1536, SIDE), value_weight, gate_weight)
    (filter_grad,) = kernel(
        "filter_grad",
        filter_kernel,
        [shape(SIDE, D, kind=F32)],
        [SMEM] + [VMEM] * 3,
        0,
        [pltpu.VMEM((CHIPS, 2, 8, 2 * SIDE), F32)],
        0.1,
        2.0,
    )(core, order, filter_part, filter_other)

    parts, input_grad, filter_grad = lax.optimization_barrier((parts, input_grad, filter_grad))
    sums = jnp.sum(parts.reshape(16, 64, D).astype(F32), axis=0).astype(BF16)
    sums = sums.reshape(4, 16, 2, 512).transpose(0, 2, 1, 3).reshape(8, 16, 512)
    final = lax.all_to_all(sums, ("z", "dp"), 0, 0, tiled=True)
    projection_grads = jnp.sum(final.astype(F32), axis=0) * SCALE
    return (input_grad.reshape(1, SIDE, D), projection_grads, filter_grad)


def solution(mesh):
    fine = Mesh(mesh.devices.reshape(4, 4, 4, 2, 2), SEQ + ("dp",))
    in_specs = (P("dp", SEQ, None), P("dp", SEQ, None), P(), P(), P(SEQ, None))
    out_specs = (P("dp", SEQ, None), P(SEQ, "dp"), P(SEQ, None))
    return jax.shard_map(local, mesh=fine, in_specs=in_specs, out_specs=out_specs, check_vma=False)
```

```python
import math

import jax
import jax.numpy as jnp
import numpy as np
from jax import lax
from jax.experimental import pallas as pl
from jax.experimental.pallas import tpu as pltpu
from jax.sharding import Mesh, PartitionSpec as P

F32 = jnp.float32
BF16 = jnp.bfloat16
D = 1024
L = 16384
SCALE = float(2 * L) ** (-0.5)
SIDE = 128
CHIPS = 64
ARRS = 3
ROWS = ARRS * 8
SEQ = ("x1", "x0", "y", "z", "c")
VMEM = pl.BlockSpec(memory_space=pltpu.VMEM)
SMEM = pl.BlockSpec(memory_space=pltpu.SMEM)


def one_hot_rows(index, width):
    return (index[:, None] == np.arange(width)[None, :]).astype(jnp.bfloat16)


def spread_order():
    index = []
    for y in range(4):
        for z in range(4):
            for core in range(2):
                low = [32 * z + 16 * core + 4 * y + s for s in range(4)]
                index += low + [2 * SIDE - 1 - d for d in low]
    return one_hot_rows(np.array(index), 2 * SIDE)


def block_order():
    index = []
    for half in range(2):
        for y in range(4):
            for zz in range(4):
                for i in range(16):
                    x, z, q = (y, zz, i) if half == 0 else (3 - y, 3 - zz, 15 - i)
                    index.append((16 * x + 4 * (q // 4) + z) * 8 + 4 * half + q % 4)
    return one_hot_rows(np.array(index), 512)


def tables():
    k = np.arange(SIDE)
    quarter = k + 0.25
    outer = 2 * math.pi / SIDE * np.outer(quarter, k)
    both = np.concatenate([np.cos(outer), -np.sin(outer)], axis=0)
    back = []
    for core in range(2):
        rows = [2 * g + (slot ^ core) for g in range(CHIPS) for slot in range(2)]
        back.append(both.T[np.array(rows)])
    twist = 2 * math.pi / L * np.outer(quarter, k)
    inner = 2 * math.pi / SIDE * np.outer(k, k)
    cos, sin = np.cos(inner), np.sin(inner)
    inner_table = np.block([[cos, -sin], [sin, cos]])
    return (
        both.astype(jnp.bfloat16),
        np.stack(back).astype(jnp.bfloat16),
        np.cos(twist).astype(np.float32),
        np.sin(twist).astype(np.float32),
        inner_table.astype(jnp.bfloat16),
        inner_table.T.astype(jnp.bfloat16),
    )


def dot(a, b, ca=1, cb=0):
    return lax.dot_general(a, b, (((ca,), (cb,)), ((), ())), preferred_element_type=F32)


def project_kernel(core, inputs, cot, taps, order, value_w, gate_w, message, cot_own, cot_give, w_buf, cot_buf, sems):
    fetch = [
        pltpu.make_async_copy(w, w_buf.at[i], sems.at[i]) for i, w in enumerate((value_w, gate_w))
    ]
    for copy in fetch:
        copy.start()
    fetch[0].wait()
    value = dot(inputs[...], w_buf[0]).astype(BF16)
    fetch[1].wait()
    gate = dot(inputs[...], w_buf[1])
    mix = (cot[...].astype(F32) * gate).astype(BF16)
    stacked = jnp.concatenate([value, mix, taps[...], cot[...]], axis=0)
    for b in range(4):
        low = stacked[:, b * SIDE:(b + 1) * SIDE]
        high = stacked[:, (7 - b) * SIDE:(8 - b) * SIDE]
        moved = dot(order[...], jnp.concatenate([low, high], axis=1), 1, 1)
        parts = [moved[:, a * SIDE:(a + 1) * SIDE].reshape(32, 8, SIDE) for a in range(4)]
        block = jnp.concatenate(parts[:3], axis=1).reshape(32 * ROWS, SIDE).astype(BF16)
        message[b * 32 * ROWS:(b + 1) * 32 * ROWS, :] = block
        line = parts[3].reshape(16, 2, 8, SIDE)
        for c in range(2):
            rows = line[:, c].reshape(SIDE, SIDE).astype(BF16)
            cot_buf[c ^ core[0], b * SIDE:(b + 1) * SIDE, :] = rows
    cot_own[...] = cot_buf[0]
    cot_give[...] = cot_buf[1]


def inverse(both, outer_tm, cos, sin, inner_tm):
    part = dot(both, inner_tm)
    re, im = part[:, :SIDE], part[:, SIDE:]
    turned = jnp.concatenate([re * cos - im * sin, re * sin + im * cos], axis=0)
    return dot(outer_tm, turned.astype(BF16)) * (1.0 / L)


def convolve_kernel(core, signal, outer, outer_t, tw_re, tw_im, inner, inner_t, result, flat, spec):
    flat[...] = signal[...].astype(F32)
    outer_m = outer[...]
    outer_tm = outer_t[core[0]]
    cos = tw_re[...]
    sin = tw_im[...]
    inner_m = inner[...]
    inner_tm = inner_t[...]

    for j in range(ROWS):
        sig = flat[pl.ds(j, SIDE, stride=ROWS), :].astype(BF16)
        part = dot(outer_m, sig)
        re, im = part[:SIDE], part[SIDE:]
        turned = jnp.concatenate([re * cos + im * sin, im * cos - re * sin], axis=1)
        spec[j] = dot(turned.astype(BF16), inner_m)

    def back(re, im):
        both = jnp.concatenate([re, im], axis=1).astype(BF16)
        return inverse(both, outer_tm, cos, sin, inner_tm)

    def mul(a, b):
        return (a[0] * b[0] - a[1] * b[1], a[0] * b[1] + a[1] * b[0])

    def mulc(a, b):
        return (a[0] * b[0] + a[1] * b[1], a[0] * b[1] - a[1] * b[0])

    def add(a, b):
        return (a[0] + b[0], a[1] + b[1])

    def load(j):
        both = spec[j]
        return (both[:, :SIDE], both[:, SIDE:])

    for s in range(8):
        t = (s + 4) % 8
        vals, grads, filt = load(s), load(8 + s), load(16 + s)
        vals_f, grads_f, filt_f = load(t), load(8 + t), load(16 + t)
        mixed = back(*add(mul(filt, vals), mulc(filt, vals_f)))
        flat[pl.ds(s, SIDE, stride=ROWS), :] = mixed
        grad = back(*add(mulc(filt, grads), mul(filt_f, grads_f)))
        flat[pl.ds(8 + s, SIDE, stride=ROWS), :] = grad
        part = add(mulc(vals, grads), mulc(grads, vals_f))
        flat[pl.ds(16 + s, SIDE, stride=ROWS), :] = back(*part)
    result[...] = flat[...].astype(BF16)


def gate_kernel(odd, home, blocks, cot_own, cot_other, keep, send):
    full = home[...].astype(F32).reshape(CHIPS, 2 * ROWS, SIDE)
    grads, gates = [], []
    for slot, cot in enumerate((cot_own, cot_other)):
        base = slot * ROWS
        mixed = full[:, base:base + 8].reshape(512, SIDE)
        grads.append(full[:, base + 8:base + 16].reshape(512, SIDE).astype(BF16))
        gates.append((mixed * cot[...].astype(F32)).astype(BF16))
    for a, group in enumerate((grads, gates)):
        rows = dot(blocks[...], jnp.concatenate(group, axis=1))
        low, high = rows[:256], rows[256:]
        keep[a * 256:(a + 1) * 256, :] = jnp.where(odd[0] == 1, high, low).astype(BF16)
        send[a * 256:(a + 1) * 256, :] = jnp.where(odd[0] == 1, low, high).astype(BF16)


def weights_kernel(odd, mine, theirs, inputs, in_other, next_in, next_other, partial):
    total = 0.0
    for rows, one, two in ((mine, inputs, in_other), (theirs, next_in, next_other)):
        first = jnp.where(odd[0] == 1, two[...], one[...])
        second = jnp.where(odd[0] == 1, one[...], two[...])
        total = total + dot(rows[...], jnp.concatenate([first, second], axis=0))
    partial[...] = total.astype(BF16)


def natural_order(stack, order):
    width = stack.shape[3]
    low, high = [], []
    for b in range(4):
        rows = stack[16 * b:16 * b + 16].reshape(2 * SIDE, width).astype(BF16)
        both = dot(rows, order[...], 0, 0)
        low.append(both[:, :SIDE])
        high.insert(0, both[:, SIDE:])
    return jnp.concatenate(low + high, axis=1)


def inputs_kernel(core, cot, order, own, far, value_w, gate_w, input_grad, w_buf, stack, sems):
    fetch = [
        pltpu.make_async_copy(w, w_buf.at[i], sems.at[i]) for i, w in enumerate((value_w, gate_w))
    ]
    for copy in fetch:
        copy.start()
    for side, ref in ((0, own), (1, far)):
        full = ref[...].astype(F32).reshape(CHIPS, ROWS, SIDE)
        stack[:, core[0] ^ side] = jnp.concatenate([full[:, :8], full[:, 8:16]], axis=2)
    natural = natural_order(stack, order)
    gated = (natural[:SIDE] * cot[...].astype(F32)).astype(BF16)
    grad = natural[SIDE:].astype(BF16)
    fetch[0].wait()
    total = dot(grad, w_buf[0], 1, 1)
    fetch[1].wait()
    input_grad[...] = (total + dot(gated, w_buf[1], 1, 1)).astype(BF16)


def filter_kernel(core, order, mine, theirs, filter_grad, stack):
    total = (mine[...].astype(F32) + theirs[...].astype(F32)).reshape(2, CHIPS, 8, SIDE)
    for side in range(2):
        rounded = total[side].astype(BF16).astype(F32)
        stack[:, core[0] ^ side] = jnp.concatenate([rounded, total[side] - rounded], axis=2)
    both = natural_order(stack, order)
    filter_grad[...] = (both[:SIDE] + both[SIDE:]) * SCALE


def shape(*dims, kind=BF16):
    return jax.ShapeDtypeStruct(dims, kind)


def swap_cores(a):
    return lax.ppermute(a, "c", [(0, 1), (1, 0)])


def kernel(name, body, outs, ins, anys=0, scratch=(), gflop=0.1, mbyte=4.0, limit=24):
    return pl.pallas_call(
        body,
        out_shape=outs,
        in_specs=ins + [pl.BlockSpec(memory_space=pl.ANY)] * anys,
        out_specs=[VMEM] * len(outs),
        scratch_shapes=scratch,
        compiler_params=pltpu.CompilerParams(vmem_limit_bytes=limit * 2**20),
        cost_estimate=pl.CostEstimate(
            flops=int(gflop * 1e9), bytes_accessed=int(mbyte * 2**20), transcendentals=0
        ),
        name=name,
    )


def pair_rows(a, cross):
    pairs = []
    for x1 in range(2):
        for x0 in range(2):
            for c in range(2):
                x_to = x0 ^ 1 if cross else x0
                c_to = c ^ x_to
                pairs.append(((2 * x1 + x0) * 2 + c, (2 * x1 + x_to) * 2 + c_to))
    return lax.ppermute(a, ("x1", "x0", "c"), pairs)


def local(inputs, cotangent, value_weight, gate_weight, filter_taps):
    core = lax.axis_index("c").astype(jnp.int32).reshape(1)
    odd = lax.axis_index("x0").astype(jnp.int32).reshape(1)
    order = jnp.asarray(spread_order())
    flat_in = inputs.reshape(SIDE, D)
    cot = cotangent.reshape(SIDE, D)
    w_scratch = pltpu.VMEM((2, D, D), BF16)
    sems = pltpu.SemaphoreType.DMA((2,))

    message, cot_own, cot_give = kernel(
        "project",
        project_kernel,
        [shape(2 * CHIPS * ROWS, SIDE), shape(512, SIDE), shape(512, SIDE)],
        [SMEM] + [VMEM] * 4,
        2,
        [w_scratch, pltpu.VMEM((2, 512, SIDE), BF16), sems],
        0.8,
        8.0,
        56,
    )(core, flat_in, cot, filter_taps, order, value_weight, gate_weight)
    spread = lax.all_to_all(message.reshape(2 * CHIPS, ROWS, SIDE), SEQ, 0, 0, tiled=True)
    cot_other = swap_cores(cot_give)
    in_other = swap_cores(flat_in)
    next_in = lax.ppermute(flat_in, "x0", [(0, 1), (1, 0)])
    next_other = swap_cores(next_in)

    (result,) = kernel(
        "convolve",
        convolve_kernel,
        [shape(2 * CHIPS * ROWS, SIDE)],
        [SMEM] + [VMEM] * 7,
        0,
        [
            pltpu.VMEM((2 * CHIPS * ROWS, SIDE), F32),
            pltpu.VMEM((ROWS, SIDE, 2 * SIDE), F32),
        ],
        1.2,
        4.0,
    )(core, spread.reshape(2 * CHIPS * ROWS, SIDE), *[jnp.asarray(t) for t in tables()])
    home = lax.all_to_all(result.reshape(CHIPS, 2 * ROWS, SIDE), SEQ[:4], 0, 0, tiled=True)

    keep, send = kernel("gate", gate_kernel, [shape(512, 256)] * 2, [SMEM] + [VMEM] * 4, gflop=0.3, mbyte=2.0)(
        odd, home.reshape(2 * CHIPS * ROWS, SIDE), jnp.asarray(block_order()), cot_own, cot_other
    )
    mine = pair_rows(keep, False)
    theirs = pair_rows(send, True)
    (partial,) = kernel(
        "weights", weights_kernel, [shape(512, D)], [SMEM] + [VMEM] * 6, gflop=0.6, mbyte=4.0, limit=56
    )(odd, mine, theirs, flat_in, in_other, next_in, next_other)
    parts = lax.all_to_all(partial, ("x1", "y"), 0, 0, tiled=True)

    own = home[:, :ROWS]
    far = swap_cores(home[:, ROWS:])
    filter_part = jnp.stack([own[:, 16:], far[:, 16:]]).reshape(1024, SIDE)
    filter_other = lax.ppermute(filter_part, "dp", [(0, 1), (1, 0)])
    (input_grad,) = kernel(
        "input_grad",
        inputs_kernel,
        [shape(SIDE, D)],
        [SMEM] + [VMEM] * 4,
        2,
        [w_scratch, pltpu.VMEM((CHIPS, 2, 8, 2 * SIDE), F32), sems],
        0.7,
        8.0,
        56,
    )(core, cot, order, own.reshape(1536, SIDE), far.reshape(1536, SIDE), value_weight, gate_weight)
    (filter_grad,) = kernel(
        "filter_grad",
        filter_kernel,
        [shape(SIDE, D, kind=F32)],
        [SMEM] + [VMEM] * 3,
        0,
        [pltpu.VMEM((CHIPS, 2, 8, 2 * SIDE), F32)],
        0.1,
        2.0,
    )(core, order, filter_part, filter_other)

    sums = jnp.sum(parts.reshape(8, 64, D).astype(F32), axis=0).astype(BF16)
    sums = sums.reshape(4, 16, 2, 512).transpose(0, 2, 1, 3).reshape(8, 16, 512)
    final = lax.all_to_all(sums, ("z", "dp"), 0, 0, tiled=True)
    projection_grads = jnp.sum(final.astype(F32), axis=0) * SCALE
    return (input_grad.reshape(1, SIDE, D), projection_grads, filter_grad)


def solution(mesh):
    fine = Mesh(mesh.devices.reshape(2, 2, 4, 4, 2, 2), SEQ + ("dp",))
    in_specs = (P("dp", SEQ, None), P("dp", SEQ, None), P(), P(), P(SEQ, None))
    out_specs = (P("dp", SEQ, None), P(SEQ, "dp"), P(SEQ, None))
    return jax.shard_map(local, mesh=fine, in_specs=in_specs, out_specs=out_specs, check_vma=False)
```

```python
import math

import jax
import jax.numpy as jnp
import numpy as np
from jax import lax
from jax.experimental import pallas as pl
from jax.experimental.pallas import tpu as pltpu
from jax.sharding import Mesh, PartitionSpec as P

F32 = jnp.float32
BF16 = jnp.bfloat16
D = 1024
L = 16384
SCALE = float(2 * L) ** (-0.5)
SIDE = 128
CHIPS = 64
ARRS = 3
ROWS = ARRS * 8
SEQ = ("x1", "x0", "y1", "y0", "z", "c")
VMEM = pl.BlockSpec(memory_space=pltpu.VMEM)
SMEM = pl.BlockSpec(memory_space=pltpu.SMEM)


def one_hot_rows(index, width):
    return (index[:, None] == np.arange(width)[None, :]).astype(jnp.bfloat16)


def spread_order():
    index = []
    for y in range(4):
        for z in range(4):
            for core in range(2):
                low = [32 * z + 16 * core + 4 * y + s for s in range(4)]
                index += low + [2 * SIDE - 1 - d for d in low]
    return one_hot_rows(np.array(index), 2 * SIDE)


def block_order():
    index = []
    for half in range(2):
        for y0 in range(2):
            for y1 in range(2):
                for zz in range(4):
                    for i in range(16):
                        y = 2 * y1 + y0
                        x, z, q = (y, zz, i) if half == 0 else (3 - y, 3 - zz, 15 - i)
                        index.append((16 * x + 4 * (q // 4) + z) * 8 + 4 * half + q % 4)
    return one_hot_rows(np.array(index), 512)


def tables():
    k = np.arange(SIDE)
    quarter = k + 0.25
    outer = 2 * math.pi / SIDE * np.outer(quarter, k)
    both = np.concatenate([np.cos(outer), -np.sin(outer)], axis=0)
    back = []
    for core in range(2):
        rows = [2 * g + (slot ^ core) for g in range(CHIPS) for slot in range(2)]
        back.append(both.T[np.array(rows)])
    twist = 2 * math.pi / L * np.outer(quarter, k)
    inner = 2 * math.pi / SIDE * np.outer(k, k)
    cos, sin = np.cos(inner), np.sin(inner)
    inner_table = np.block([[cos, -sin], [sin, cos]])
    return (
        both.astype(jnp.bfloat16),
        np.stack(back).astype(jnp.bfloat16),
        np.cos(twist).astype(np.float32),
        np.sin(twist).astype(np.float32),
        inner_table.astype(jnp.bfloat16),
        inner_table.T.astype(jnp.bfloat16),
    )


def dot(a, b, ca=1, cb=0):
    return lax.dot_general(a, b, (((ca,), (cb,)), ((), ())), preferred_element_type=F32)


def project_kernel(core, inputs, cot, taps, order, value_w, gate_w, message, cot_own, cot_give, w_buf, cot_buf, taps_buf, sems):
    fetch = [
        pltpu.make_async_copy(w, w_buf.at[i], sems.at[i]) for i, w in enumerate((value_w, gate_w))
    ]
    for copy in fetch:
        copy.start()
    def blocks_of(arrays):
        stacked = jnp.concatenate(arrays, axis=0)
        for b in range(4):
            low = stacked[:, b * SIDE:(b + 1) * SIDE]
            high = stacked[:, (7 - b) * SIDE:(8 - b) * SIDE]
            moved = dot(order[...], jnp.concatenate([low, high], axis=1), 1, 1)
            yield b, [moved[:, a * SIDE:(a + 1) * SIDE].reshape(32, 8, SIDE) for a in range(2)]

    for b, (tap, line) in blocks_of([taps[...], cot[...]]):
        taps_buf[b] = tap
        line = line.reshape(16, 2, 8, SIDE)
        for c in range(2):
            rows = line[:, c].reshape(SIDE, SIDE).astype(BF16)
            cot_buf[c ^ core[0], b * SIDE:(b + 1) * SIDE, :] = rows
    fetch[0].wait()
    value = dot(inputs[...], w_buf[0]).astype(BF16)
    fetch[1].wait()
    gate = dot(inputs[...], w_buf[1])
    mix = (cot[...].astype(F32) * gate).astype(BF16)
    for b, parts in blocks_of([value, mix]):
        block = jnp.concatenate(parts + [taps_buf[b]], axis=1).reshape(32 * ROWS, SIDE).astype(BF16)
        message[b * 32 * ROWS:(b + 1) * 32 * ROWS, :] = block
    cot_own[...] = cot_buf[0]
    cot_give[...] = cot_buf[1]


def inverse(both, outer_tm, cos, sin, inner_tm):
    part = dot(both, inner_tm)
    re, im = part[:, :SIDE], part[:, SIDE:]
    turned = jnp.concatenate([re * cos - im * sin, re * sin + im * cos], axis=0)
    return dot(outer_tm, turned.astype(BF16)) * (1.0 / L)


def convolve_kernel(core, signal, outer, outer_t, tw_re, tw_im, inner, inner_t, result, flat, spec):
    flat[...] = signal[...].astype(F32)
    outer_m = outer[...]
    outer_tm = outer_t[core[0]]
    cos = tw_re[...]
    sin = tw_im[...]
    inner_m = inner[...]
    inner_tm = inner_t[...]

    for j in range(ROWS):
        sig = flat[pl.ds(j, SIDE, stride=ROWS), :].astype(BF16)
        part = dot(outer_m, sig)
        re, im = part[:SIDE], part[SIDE:]
        turned = jnp.concatenate([re * cos + im * sin, im * cos - re * sin], axis=1)
        spec[j] = dot(turned.astype(BF16), inner_m)

    def back(re, im):
        both = jnp.concatenate([re, im], axis=1).astype(BF16)
        return inverse(both, outer_tm, cos, sin, inner_tm)

    def mul(a, b):
        return (a[0] * b[0] - a[1] * b[1], a[0] * b[1] + a[1] * b[0])

    def mulc(a, b):
        return (a[0] * b[0] + a[1] * b[1], a[0] * b[1] - a[1] * b[0])

    def add(a, b):
        return (a[0] + b[0], a[1] + b[1])

    def load(j):
        both = spec[j]
        return (both[:, :SIDE], both[:, SIDE:])

    for s in range(8):
        t = (s + 4) % 8
        vals, grads, filt = load(s), load(8 + s), load(16 + s)
        vals_f, grads_f, filt_f = load(t), load(8 + t), load(16 + t)
        mixed = back(*add(mul(filt, vals), mulc(filt, vals_f)))
        flat[pl.ds(s, SIDE, stride=ROWS), :] = mixed
        grad = back(*add(mulc(filt, grads), mul(filt_f, grads_f)))
        flat[pl.ds(8 + s, SIDE, stride=ROWS), :] = grad
        part = add(mulc(vals, grads), mulc(grads, vals_f))
        flat[pl.ds(16 + s, SIDE, stride=ROWS), :] = back(*part)
    result[...] = flat[...].astype(BF16)


def gate_kernel(odd, home, blocks, cot_own, cot_other, *outs):
    full = home[...].astype(F32).reshape(CHIPS, 2 * ROWS, SIDE)
    grads, gates = [], []
    for slot, cot in enumerate((cot_own, cot_other)):
        base = slot * ROWS
        mixed = full[:, base:base + 8].reshape(512, SIDE)
        grads.append(full[:, base + 8:base + 16].reshape(512, SIDE).astype(BF16))
        gates.append((mixed * cot[...].astype(F32)).astype(BF16))
    for a, group in enumerate((grads, gates)):
        rows = dot(blocks[...], jnp.concatenate(group, axis=1))
        parts = [[rows[(2 * h + q) * SIDE:(2 * h + q + 1) * SIDE] for q in range(2)] for h in range(2)]
        for dx in range(2):
            line = [jnp.where(odd[0] == 1, parts[1 - dx][q], parts[dx][q]) for q in range(2)]
            for dy in range(2):
                part = jnp.where(odd[1] == 1, line[1 - dy], line[dy])
                outs[2 * dx + dy][a * SIDE:(a + 1) * SIDE, :] = part.astype(BF16)


def weights_kernel(odd, *refs):
    rows, ins, partial = refs[:4], refs[4:12], refs[12]
    total = 0.0
    for k in range(4):
        one, two = ins[2 * k][...], ins[2 * k + 1][...]
        first = jnp.where(odd[0] == 1, two, one)
        second = jnp.where(odd[0] == 1, one, two)
        total = total + dot(rows[k][...], jnp.concatenate([first, second], axis=0))
    for half in range(2):
        cols = total[:, half * 512:(half + 1) * 512].astype(BF16)
        partial[:, half] = cols.reshape(16, 16, 512)


def natural_order(stack, order):
    width = stack.shape[3]
    low, high = [], []
    for b in range(4):
        rows = stack[16 * b:16 * b + 16].reshape(2 * SIDE, width).astype(BF16)
        both = dot(rows, order[...], 0, 0)
        low.append(both[:, :SIDE])
        high.insert(0, both[:, SIDE:])
    return jnp.concatenate(low + high, axis=1)


def inputs_kernel(core, cot, order, home, far, value_w, gate_w, input_grad, w_buf, stack, sems):
    fetch = [
        pltpu.make_async_copy(w, w_buf.at[i], sems.at[i]) for i, w in enumerate((value_w, gate_w))
    ]
    for copy in fetch:
        copy.start()
    near = home[...].astype(F32).reshape(CHIPS, 2 * ROWS, SIDE)
    other = far[...].astype(F32).reshape(CHIPS, 16, SIDE)
    for side, full in ((0, near), (1, other)):
        stack[:, core[0] ^ side] = jnp.concatenate([full[:, :8], full[:, 8:16]], axis=2)
    natural = natural_order(stack, order)
    gated = (natural[:SIDE] * cot[...].astype(F32)).astype(BF16)
    grad = natural[SIDE:].astype(BF16)
    fetch[0].wait()
    total = dot(grad, w_buf[0], 1, 1)
    fetch[1].wait()
    input_grad[...] = (total + dot(gated, w_buf[1], 1, 1)).astype(BF16)


def filter_kernel(core, order, own, far, filter_grad, stack):
    for side, ref in ((0, own), (1, far)):
        stack[:, core[0] ^ side] = ref[...].astype(F32).reshape(CHIPS, 8, SIDE)
    filter_grad[...] = natural_order(stack, order) * SCALE


def shape(*dims, kind=BF16):
    return jax.ShapeDtypeStruct(dims, kind)


def swap_cores(a):
    return lax.ppermute(a, "c", [(0, 1), (1, 0)])


def kernel(name, body, outs, ins, anys=0, scratch=(), gflop=0.1, mbyte=4.0, limit=24):
    return pl.pallas_call(
        body,
        out_shape=outs,
        in_specs=ins + [pl.BlockSpec(memory_space=pl.ANY)] * anys,
        out_specs=[VMEM] * len(outs),
        scratch_shapes=scratch,
        compiler_params=pltpu.CompilerParams(vmem_limit_bytes=limit * 2**20),
        cost_estimate=pl.CostEstimate(
            flops=int(gflop * 1e9), bytes_accessed=int(mbyte * 2**20), transcendentals=0
        ),
        name=name,
    )


def near(a, dx, dy, cross=False):
    pairs = []
    for x0 in range(2):
        for y1 in range(2):
            for y0 in range(2):
                for z in range(4):
                    for c in range(2):
                        x_to = x0 ^ dx
                        c_to = c ^ x_to if cross else c
                        start = (((2 * x0 + y1) * 2 + y0) * 4 + z) * 2 + c
                        pairs.append((start, (((2 * x_to + y1) * 2 + (y0 ^ dy)) * 4 + z) * 2 + c_to))
    return lax.ppermute(a, ("x0", "y1", "y0", "z", "c"), pairs)


def local(inputs, cotangent, value_weight, gate_weight, filter_taps):
    core = lax.axis_index("c").astype(jnp.int32).reshape(1)
    odd = jnp.stack([lax.axis_index(name).astype(jnp.int32) for name in ("x0", "y0")])
    order = jnp.asarray(spread_order())
    flat_in = inputs.reshape(SIDE, D)
    cot = cotangent.reshape(SIDE, D)
    w_scratch = pltpu.VMEM((2, D, D), BF16)
    sems = pltpu.SemaphoreType.DMA((2,))

    message, cot_own, cot_give = kernel(
        "project",
        project_kernel,
        [shape(2 * CHIPS * ROWS, SIDE), shape(512, SIDE), shape(512, SIDE)],
        [SMEM] + [VMEM] * 4,
        2,
        [w_scratch, pltpu.VMEM((2, 512, SIDE), BF16), pltpu.VMEM((4, 32, 8, SIDE), F32), sems],
        0.8,
        8.0,
        56,
    )(core, flat_in, cot, filter_taps, order, value_weight, gate_weight)
    spread = lax.all_to_all(message.reshape(2 * CHIPS, ROWS, SIDE), SEQ, 0, 0, tiled=True)
    cot_other = swap_cores(cot_give)
    ins = []
    for dx in range(2):
        for dy in range(2):
            block = near(flat_in, dx, dy) if dx + dy else flat_in
            ins += [block, swap_cores(block)]

    (result,) = kernel(
        "convolve",
        convolve_kernel,
        [shape(2 * CHIPS * ROWS, SIDE)],
        [SMEM] + [VMEM] * 7,
        0,
        [
            pltpu.VMEM((2 * CHIPS * ROWS, SIDE), F32),
            pltpu.VMEM((ROWS, SIDE, 2 * SIDE), F32),
        ],
        1.2,
        4.0,
    )(core, spread.reshape(2 * CHIPS * ROWS, SIDE), *[jnp.asarray(t) for t in tables()])
    home = lax.all_to_all(result.reshape(CHIPS, 2 * ROWS, SIDE), SEQ[:5], 0, 0, tiled=True)

    rows = kernel("gate", gate_kernel, [shape(256, 256)] * 4, [SMEM] + [VMEM] * 4, gflop=0.3, mbyte=2.0)(
        odd, home.reshape(2 * CHIPS * ROWS, SIDE), jnp.asarray(block_order()), cot_own, cot_other
    )
    shaped = home.reshape(CHIPS, 2, ROWS, SIDE)
    filter_part = jnp.stack([shaped[:, slot, 16:] for slot in range(2)])
    cuts = filter_part.reshape(2, 64, 8, SIDE)
    cuts = [cuts[i] for i in range(2)]
    cuts, rows = lax.optimization_barrier((cuts, rows))
    others = [lax.ppermute(cut, "dp", [(0, 1), (1, 0)]) for cut in cuts]
    sums = [(cut.astype(F32) + other.astype(F32)).astype(BF16) for cut, other in zip(cuts, others)]
    filter_sum = jnp.concatenate(sums, axis=0).reshape(2, CHIPS, 8, SIDE)
    rows = [near(rows[2 * dx + dy], dx, dy, True) for dx in range(2) for dy in range(2)]
    (partial,) = kernel(
        "weights", weights_kernel, [shape(16, 2, 16, 512)], [SMEM] + [VMEM] * 12, gflop=0.6, mbyte=4.0, limit=56
    )(odd, *rows, *ins)
    parts = lax.all_to_all(partial.reshape(4, SIDE, 512), ("x1", "y1"), 0, 0, tiled=True)

    far = swap_cores(shaped[:, 1, :16])
    filter_far = swap_cores(filter_sum[1])
    (input_grad,) = kernel(
        "input_grad",
        inputs_kernel,
        [shape(SIDE, D)],
        [SMEM] + [VMEM] * 4,
        2,
        [w_scratch, pltpu.VMEM((CHIPS, 2, 8, 2 * SIDE), F32), sems],
        0.7,
        8.0,
        56,
    )(core, cot, order, home.reshape(3072, SIDE), far.reshape(1024, SIDE), value_weight, gate_weight)
    (filter_grad,) = kernel(
        "filter_grad",
        filter_kernel,
        [shape(SIDE, D, kind=F32)],
        [SMEM] + [VMEM] * 3,
        0,
        [pltpu.VMEM((CHIPS, 2, 8, SIDE), F32)],
        0.1,
        2.0,
    )(core, order, filter_sum[0].reshape(512, SIDE), filter_far.reshape(512, SIDE))

    rows = jnp.sum(parts.astype(F32), axis=0).astype(BF16).reshape(8, 16, 512)
    final = lax.all_to_all(rows, ("z", "dp"), 0, 0, tiled=True)
    projection_grads = jnp.sum(final.astype(F32), axis=0) * SCALE
    return (input_grad.reshape(1, SIDE, D), projection_grads, filter_grad)


def solution(mesh):
    fine = Mesh(mesh.devices.reshape(2, 2, 2, 2, 4, 2, 2), SEQ + ("dp",))
    in_specs = (P("dp", SEQ, None), P("dp", SEQ, None), P(), P(), P(SEQ, None))
    out_specs = (P("dp", SEQ, None), P(SEQ, "dp"), P(SEQ, None))
    return jax.shard_map(local, mesh=fine, in_specs=in_specs, out_specs=out_specs, check_vma=False)
```

```python
import math

import jax
import jax.numpy as jnp
import numpy as np
from jax import lax
from jax.experimental import pallas as pl
from jax.experimental.pallas import tpu as pltpu
from jax.sharding import Mesh, PartitionSpec as P

F32 = jnp.float32
BF16 = jnp.bfloat16
D = 1024
L = 16384
SCALE = float(2 * L) ** (-0.5)
SIDE = 128
CHIPS = 64
ARRS = 3
ROWS = ARRS * 8
SEQ = ("x1", "x0", "y1", "y0", "z", "c")
VMEM = pl.BlockSpec(memory_space=pltpu.VMEM)
SMEM = pl.BlockSpec(memory_space=pltpu.SMEM)


def one_hot_rows(index, width):
    return (index[:, None] == np.arange(width)[None, :]).astype(jnp.bfloat16)


def spread_order():
    index = []
    for y in range(4):
        for z in range(4):
            for core in range(2):
                low = [32 * z + 16 * core + 4 * y + s for s in range(4)]
                index += low + [2 * SIDE - 1 - d for d in low]
    return one_hot_rows(np.array(index), 2 * SIDE)


def block_order():
    index = []
    for half in range(2):
        for y in range(4):
            for zz in range(4):
                for i in range(16):
                    x, z, q = (y, zz, i) if half == 0 else (3 - y, 3 - zz, 15 - i)
                    index.append((16 * x + 4 * (q // 4) + z) * 8 + 4 * half + q % 4)
    return one_hot_rows(np.array(index), 512)


def tables():
    k = np.arange(SIDE)
    quarter = k + 0.25
    outer = 2 * math.pi / SIDE * np.outer(quarter, k)
    both = np.concatenate([np.cos(outer), -np.sin(outer)], axis=0)
    back = []
    for core in range(2):
        rows = [2 * g + (slot ^ core) for g in range(CHIPS) for slot in range(2)]
        back.append(both.T[np.array(rows)])
    twist = 2 * math.pi / L * np.outer(quarter, k)
    inner = 2 * math.pi / SIDE * np.outer(k, k)
    cos, sin = np.cos(inner), np.sin(inner)
    inner_table = np.block([[cos, -sin], [sin, cos]])
    return (
        both.astype(jnp.bfloat16),
        np.stack(back).astype(jnp.bfloat16),
        np.cos(twist).astype(np.float32),
        np.sin(twist).astype(np.float32),
        inner_table.astype(jnp.bfloat16),
        inner_table.T.astype(jnp.bfloat16),
    )


def dot(a, b, ca=1, cb=0):
    return lax.dot_general(a, b, (((ca,), (cb,)), ((), ())), preferred_element_type=F32)


def project_kernel(core, inputs, cot, taps, order, value_w, gate_w, message, cot_own, cot_give, w_buf, cot_buf, taps_buf, sems):
    fetch = [
        pltpu.make_async_copy(w, w_buf.at[i], sems.at[i]) for i, w in enumerate((value_w, gate_w))
    ]
    for copy in fetch:
        copy.start()
    def blocks_of(arrays):
        stacked = jnp.concatenate(arrays, axis=0)
        for b in range(4):
            low = stacked[:, b * SIDE:(b + 1) * SIDE]
            high = stacked[:, (7 - b) * SIDE:(8 - b) * SIDE]
            moved = dot(order[...], jnp.concatenate([low, high], axis=1), 1, 1)
            yield b, [moved[:, a * SIDE:(a + 1) * SIDE].reshape(32, 8, SIDE) for a in range(2)]

    for b, (tap, line) in blocks_of([taps[...], cot[...]]):
        taps_buf[b] = tap
        line = line.reshape(16, 2, 8, SIDE)
        for c in range(2):
            rows = line[:, c].reshape(SIDE, SIDE).astype(BF16)
            cot_buf[c ^ core[0], b * SIDE:(b + 1) * SIDE, :] = rows
    fetch[0].wait()
    value = dot(inputs[...], w_buf[0]).astype(BF16)
    fetch[1].wait()
    gate = dot(inputs[...], w_buf[1])
    mix = (cot[...].astype(F32) * gate).astype(BF16)
    for b, parts in blocks_of([value, mix]):
        block = jnp.concatenate(parts + [taps_buf[b]], axis=1).reshape(32 * ROWS, SIDE).astype(BF16)
        message[b * 32 * ROWS:(b + 1) * 32 * ROWS, :] = block
    cot_own[...] = cot_buf[0]
    cot_give[...] = cot_buf[1]


def inverse(both, outer_tm, cos, sin, inner_tm):
    part = dot(both, inner_tm)
    re, im = part[:, :SIDE], part[:, SIDE:]
    turned = jnp.concatenate([re * cos - im * sin, re * sin + im * cos], axis=0)
    return dot(outer_tm, turned.astype(BF16)) * (1.0 / L)


def convolve_kernel(core, signal, outer, outer_t, tw_re, tw_im, inner, inner_t, result, flat, spec):
    flat[...] = signal[...].astype(F32)
    outer_m = outer[...]
    outer_tm = outer_t[core[0]]
    cos = tw_re[...]
    sin = tw_im[...]
    inner_m = inner[...]
    inner_tm = inner_t[...]

    for j in range(ROWS):
        sig = flat[pl.ds(j, SIDE, stride=ROWS), :].astype(BF16)
        part = dot(outer_m, sig)
        re, im = part[:SIDE], part[SIDE:]
        turned = jnp.concatenate([re * cos + im * sin, im * cos - re * sin], axis=1)
        spec[j] = dot(turned.astype(BF16), inner_m)

    def back(re, im):
        both = jnp.concatenate([re, im], axis=1).astype(BF16)
        return inverse(both, outer_tm, cos, sin, inner_tm)

    def mul(a, b):
        return (a[0] * b[0] - a[1] * b[1], a[0] * b[1] + a[1] * b[0])

    def mulc(a, b):
        return (a[0] * b[0] + a[1] * b[1], a[0] * b[1] - a[1] * b[0])

    def add(a, b):
        return (a[0] + b[0], a[1] + b[1])

    def load(j):
        both = spec[j]
        return (both[:, :SIDE], both[:, SIDE:])

    for s in range(8):
        t = (s + 4) % 8
        vals, grads, filt = load(s), load(8 + s), load(16 + s)
        vals_f, grads_f, filt_f = load(t), load(8 + t), load(16 + t)
        mixed = back(*add(mul(filt, vals), mulc(filt, vals_f)))
        flat[pl.ds(s, SIDE, stride=ROWS), :] = mixed
        grad = back(*add(mulc(filt, grads), mul(filt_f, grads_f)))
        flat[pl.ds(8 + s, SIDE, stride=ROWS), :] = grad
        part = add(mulc(vals, grads), mulc(grads, vals_f))
        flat[pl.ds(16 + s, SIDE, stride=ROWS), :] = back(*part)
    result[...] = flat[...].astype(BF16)


def gate_kernel(odd, home, blocks, cot_own, cot_other, *outs):
    full = home[...].astype(F32).reshape(CHIPS, 2 * ROWS, SIDE)
    grads, gates = [], []
    for slot, cot in enumerate((cot_own, cot_other)):
        base = slot * ROWS
        mixed = full[:, base:base + 8].reshape(512, SIDE)
        grads.append(full[:, base + 8:base + 16].reshape(512, SIDE).astype(BF16))
        gates.append((mixed * cot[...].astype(F32)).astype(BF16))
    parts = []
    for group in (grads, gates):
        rows = dot(blocks[...], jnp.concatenate(group, axis=1))
        parts.append((rows[:256], rows[256:]))
    for far_x in range(2):
        line = [jnp.where(odd[1] == 1, parts[1 - far_x][h], parts[far_x][h]) for h in range(2)]
        for dx in range(2):
            part = jnp.where(odd[0] == 1, line[1 - dx], line[dx])
            outs[2 * far_x + dx][...] = part.astype(BF16)


def weights_kernel(odd, *refs):
    rows, ins, partial = refs[:4], refs[4:12], refs[12]
    total = 0.0
    for k in range(4):
        one, two = ins[2 * k][...], ins[2 * k + 1][...]
        first = jnp.where(odd[0] == 1, two, one)
        second = jnp.where(odd[0] == 1, one, two)
        total = total + dot(rows[k][...], jnp.concatenate([first, second], axis=0))
    for half in range(2):
        cols = total[:, half * 512:(half + 1) * 512].astype(BF16)
        partial[:, half] = cols.reshape(16, 16, 512)


def natural_order(stack, order):
    width = stack.shape[3]
    low, high = [], []
    for b in range(4):
        rows = stack[16 * b:16 * b + 16].reshape(2 * SIDE, width).astype(BF16)
        both = dot(rows, order[...], 0, 0)
        low.append(both[:, :SIDE])
        high.insert(0, both[:, SIDE:])
    return jnp.concatenate(low + high, axis=1)


def natural_kernel(core, cot, order, home, far, rows, stack):
    near = home[...].astype(F32).reshape(CHIPS, 2 * ROWS, SIDE)
    other = far[...].astype(F32).reshape(CHIPS, 16, SIDE)
    for side, full in ((0, near), (1, other)):
        stack[:, core[0] ^ side] = jnp.concatenate([full[:, :8], full[:, 8:16]], axis=2)
    natural = natural_order(stack, order)
    rows[:SIDE, :] = (natural[:SIDE] * cot[...].astype(F32)).astype(BF16)
    rows[SIDE:, :] = natural[SIDE:].astype(BF16)


def inputs_kernel(rows, value_w, gate_w, input_grad, w_buf, sems):
    fetch = [
        pltpu.make_async_copy(w, w_buf.at[i], sems.at[i]) for i, w in enumerate((value_w, gate_w))
    ]
    for copy in fetch:
        copy.start()
    fetch[0].wait()
    total = dot(rows[SIDE:, :], w_buf[0], 1, 1)
    fetch[1].wait()
    input_grad[...] = (total + dot(rows[:SIDE, :], w_buf[1], 1, 1)).astype(BF16)


def filter_kernel(core, order, own, far, filter_grad, stack):
    for side, ref in ((0, own), (1, far)):
        stack[:, core[0] ^ side] = ref[...].astype(F32).reshape(CHIPS, 8, SIDE)
    filter_grad[...] = natural_order(stack, order) * SCALE


def shape(*dims, kind=BF16):
    return jax.ShapeDtypeStruct(dims, kind)


def swap_cores(a):
    return lax.ppermute(a, "c", [(0, 1), (1, 0)])


def kernel(name, body, outs, ins, anys=0, scratch=(), gflop=0.1, mbyte=4.0, limit=24):
    return pl.pallas_call(
        body,
        out_shape=outs,
        in_specs=ins + [pl.BlockSpec(memory_space=pl.ANY)] * anys,
        out_specs=[VMEM] * len(outs),
        scratch_shapes=scratch,
        compiler_params=pltpu.CompilerParams(vmem_limit_bytes=limit * 2**20),
        cost_estimate=pl.CostEstimate(
            flops=int(gflop * 1e9), bytes_accessed=int(mbyte * 2**20), transcendentals=0
        ),
        name=name,
    )


def near(a, far_x, dx, cross=False):
    pairs = []
    for x in range(4):
        for c in range(2):
            x_to = x ^ (2 * far_x + dx)
            c_to = c ^ (x_to & 1) if cross else c
            pairs.append((2 * x + c, 2 * x_to + c_to))
    return lax.ppermute(a, ("x1", "x0", "c"), pairs)


def local(inputs, cotangent, value_weight, gate_weight, filter_taps):
    core = lax.axis_index("c").astype(jnp.int32).reshape(1)
    odd = jnp.stack([lax.axis_index(name).astype(jnp.int32) for name in ("x0", "x1")])
    order = jnp.asarray(spread_order())
    flat_in = inputs.reshape(SIDE, D)
    cot = cotangent.reshape(SIDE, D)
    w_scratch = pltpu.VMEM((2, D, D), BF16)
    sems = pltpu.SemaphoreType.DMA((2,))

    message, cot_own, cot_give = kernel(
        "project",
        project_kernel,
        [shape(2 * CHIPS * ROWS, SIDE), shape(512, SIDE), shape(512, SIDE)],
        [SMEM] + [VMEM] * 4,
        2,
        [w_scratch, pltpu.VMEM((2, 512, SIDE), BF16), pltpu.VMEM((4, 32, 8, SIDE), F32), sems],
        0.8,
        8.0,
        56,
    )(core, flat_in, cot, filter_taps, order, value_weight, gate_weight)
    spread = lax.all_to_all(message.reshape(2 * CHIPS, ROWS, SIDE), SEQ, 0, 0, tiled=True)
    cot_other = swap_cores(cot_give)
    ins = []
    for dx in range(2):
        for dy in range(2):
            block = near(flat_in, dx, dy) if dx + dy else flat_in
            ins += [block, swap_cores(block)]

    (result,) = kernel(
        "convolve",
        convolve_kernel,
        [shape(2 * CHIPS * ROWS, SIDE)],
        [SMEM] + [VMEM] * 7,
        0,
        [
            pltpu.VMEM((2 * CHIPS * ROWS, SIDE), F32),
            pltpu.VMEM((ROWS, SIDE, 2 * SIDE), F32),
        ],
        1.2,
        4.0,
    )(core, spread.reshape(2 * CHIPS * ROWS, SIDE), *[jnp.asarray(t) for t in tables()])
    home = lax.all_to_all(result.reshape(CHIPS, 2 * ROWS, SIDE), SEQ[:5], 0, 0, tiled=True)

    rows = kernel("gate", gate_kernel, [shape(256, 256)] * 4, [SMEM] + [VMEM] * 4, gflop=0.3, mbyte=2.0)(
        odd, home.reshape(2 * CHIPS * ROWS, SIDE), jnp.asarray(block_order()), cot_own, cot_other
    )
    shaped = home.reshape(CHIPS, 2, ROWS, SIDE)
    filter_part = jnp.stack([shaped[:, slot, 16:] for slot in range(2)])
    cuts = filter_part.reshape(2, 64, 8, SIDE)
    cuts = [cuts[i] for i in range(2)]
    cuts, rows = lax.optimization_barrier((cuts, rows))
    others = [lax.ppermute(cut, "dp", [(0, 1), (1, 0)]) for cut in cuts]
    sums = [(cut.astype(F32) + other.astype(F32)).astype(BF16) for cut, other in zip(cuts, others)]
    filter_sum = jnp.concatenate(sums, axis=0).reshape(2, CHIPS, 8, SIDE)
    rows = [near(rows[2 * dx + dy], dx, dy, True) for dx in range(2) for dy in range(2)]
    (partial,) = kernel(
        "weights", weights_kernel, [shape(16, 2, 16, 512)], [SMEM] + [VMEM] * 12, gflop=0.6, mbyte=4.0, limit=20
    )(odd, *rows, *ins)
    parts = lax.all_to_all(partial.reshape(4, SIDE, 512), ("y1", "y0"), 0, 0, tiled=True)

    far = swap_cores(shaped[:, 1, :16])
    filter_far = swap_cores(filter_sum[1])
    (natural,) = kernel(
        "natural",
        natural_kernel,
        [shape(2 * SIDE, D)],
        [SMEM] + [VMEM] * 4,
        0,
        [pltpu.VMEM((CHIPS, 2, 8, 2 * SIDE), F32)],
        0.2,
        3.0,
    )(core, cot, order, home.reshape(3072, SIDE), far.reshape(1024, SIDE))
    parts, natural = lax.optimization_barrier((parts, natural))
    (input_grad,) = kernel(
        "input_grad",
        inputs_kernel,
        [shape(SIDE, D)],
        [VMEM],
        2,
        [w_scratch, sems],
        0.6,
        8.0,
        56,
    )(natural, value_weight, gate_weight)
    (filter_grad,) = kernel(
        "filter_grad",
        filter_kernel,
        [shape(SIDE, D, kind=F32)],
        [SMEM] + [VMEM] * 3,
        0,
        [pltpu.VMEM((CHIPS, 2, 8, SIDE), F32)],
        0.1,
        2.0,
    )(core, order, filter_sum[0].reshape(512, SIDE), filter_far.reshape(512, SIDE))

    rows = jnp.sum(parts.astype(F32), axis=0).astype(BF16).reshape(8, 16, 512)
    final = lax.all_to_all(rows, ("z", "dp"), 0, 0, tiled=True)
    projection_grads = jnp.sum(final.astype(F32), axis=0) * SCALE
    return (input_grad.reshape(1, SIDE, D), projection_grads, filter_grad)


def solution(mesh):
    fine = Mesh(mesh.devices.reshape(2, 2, 2, 2, 4, 2, 2), SEQ + ("dp",))
    in_specs = (P("dp", SEQ, None), P("dp", SEQ, None), P(), P(), P(SEQ, None))
    out_specs = (P("dp", SEQ, None), P(SEQ, "dp"), P(SEQ, None))
    return jax.shard_map(local, mesh=fine, in_specs=in_specs, out_specs=out_specs, check_vma=False)
```
